512 devices in a mesh: section: 16 (over x, y_hi, core), tensor: 32 (over z, y_lo).
Axes of the slice: x: 4, y: 4 (y_hi: 2, y_lo: 2; y = y_hi * 2 + y_lo), z: 16, core: 2. Of those that a mesh axis runs over, the one named last changes fastest.
Arguments:
- hidden: bfloat16 [1024, 8192], P('section', 'tensor'), may hold values from -30 to 30
- audio: bfloat16 [512, 8192], P('section', 'tensor'), may hold values from -30 to 30
- audio_dest: int32 [512, 1], replicated, may hold values from 0 to 15; in each aligned block of 32 rows (0 to 31, 32 to 63, ...) at most 4 rows name the same one
- segment: int32 [32, 64], replicated, may hold values from 0 to 3, never falling along the last dimension, each value on 1 to 32 neighbouring positions
- norm_gain: bfloat16 [16, 8192], P('section', 'tensor'), may hold values from 0.25 to 1.75
- w_query: bfloat16 [16, 8192, 4096], P('section', None, 'tensor'), may hold values from -1 to 1
- w_keyval: bfloat16 [16, 8192, 1024], P('section', 'tensor'), may hold values from -1 to 1
- w_out: bfloat16 [16, 4096, 8192], P('section', None, 'tensor'), may hold values from -0.09375 to 0.09375
Outputs:
- lap_state: bfloat16 [2048, 8192], P('section', 'tensor')
The draws below stay inside these ranges and needn't reach their ends.
Inputs may be any that keep to these rules, and one draw needn't show every extreme that they name: `audio_dest`: in each aligned block of 32 rows (the audio rows of one stop) no stop is named more than 4 times, a bound that some block reaches.
All inputs are finite; a program needn't handle non-finite values.
Results may differ from the reference program's by a relative error of at most 0.018.
Values may be sent and summed in bfloat16 or wider, within the bound.
No kernel may reach another device: no remote copies, remote signals or barrier semaphores. Data moves between devices by JAX's collectives and lax.ppermute only.
A program may use at most 64 MiB of HBM per device.

```python
import math
import jax
import jax.numpy as jnp
import numpy as np
from jax import lax

D = 8192
HD = 128
KVH = 4
MB_DEV = 2
AUD_MB = 32
TXT_MB = 32
AUD_DEV = 32
STEPS = 4
HEADS = 32
MB_ROWS = 64
CAP = 4
N_SECTION = 16


def spread_scales(key, rows):
    first, second = jax.random.split(key)
    row_scale = jnp.exp(jax.random.uniform(first, (rows, 1)) * math.log(10.0))
    ramp = 3.0 ** (jnp.arange(D, dtype=jnp.float32) / (D - 1))
    col_scale = jnp.exp(jax.random.uniform(second, (1, D)) * math.log(10.0 / 3.0)) * ramp
    return (row_scale, col_scale)


def draw_hidden(key, part):
    key = jax.random.fold_in(key, 11)
    rows = N_SECTION * MB_DEV * TXT_MB
    key_scale, key_noise = jax.random.split(key, 2)
    row_scale, col_scale = spread_scales(key_scale, rows)
    base = jnp.clip(jax.random.normal(key_noise, (rows, D)), -6.0, 6.0)
    return (0.02 * base * row_scale * col_scale).astype(jnp.bfloat16)


def draw_audio(key, part):
    key = jax.random.fold_in(key, 12)
    rows = N_SECTION * AUD_DEV
    key_scale, key_noise = jax.random.split(key, 2)
    row_scale, col_scale = spread_scales(key_scale, rows)
    base = jnp.clip(jax.random.normal(key_noise, (rows, D)), -6.0, 6.0)
    return (0.02 * base * row_scale * col_scale).astype(jnp.bfloat16)


def draw_w_query(key, part):
    key = jax.random.fold_in(key, 21)
    key_noise = jax.random.fold_in(key, 0)
    group = HEADS // KVH
    values = jnp.clip(jax.random.normal(key_noise, (N_SECTION, D, KVH, group, HD)), -6.0, 6.0)
    scaled = jnp.clip(values / math.sqrt(D), -1.0, 1.0)
    return scaled.reshape(N_SECTION, D, HEADS * HD).astype(jnp.bfloat16)


def draw_w_keyval(key, part):
    key = jax.random.fold_in(key, 22)
    key_first, key_second = jax.random.split(key)
    value_part = jnp.clip(jax.random.normal(key_second, (N_SECTION, D, KVH, HD)), -6.0, 6.0)
    key_part = jnp.clip(jax.random.normal(key_first, (N_SECTION, D, KVH, HD)), -6.0, 6.0)
    both = jnp.stack([key_part, value_part], axis=3)
    scaled = jnp.clip(both / math.sqrt(D), -1.0, 1.0)
    return scaled.reshape(N_SECTION, D, KVH * 2 * HD).astype(jnp.bfloat16)


def level_of(own_key, extent, cuts, least, top_value):
    def one(dim, shards_of):
        heights = jax.random.uniform(jax.random.fold_in(jax.random.fold_in(own_key, 6), dim), (shards_of,), jnp.float32, least / len(cuts), top_value / len(cuts))
        return jnp.repeat(jnp.exp(heights), extent[dim] // shards_of).reshape((-1,) + (1,) * (len(extent) - dim - 1))

    factor_of = one(*cuts[0])
    for cut in cuts[1:]:
        factor_of = factor_of * one(*cut)
    return factor_of


def length_profile(number_of, total, most, skew):
    loads = [(1 << 20) // math.isqrt(grade ** skew) + 1 for grade in range(2, number_of + 1)]
    surplus, counts = total - most - (number_of - 1), [1] * (number_of - 1)
    while surplus > 0:
        candidates = [i for i in range(number_of - 1) if counts[i] < most]
        mass, budget = sum([loads[i] for i in candidates]), surplus
        for i in candidates:
            more = min(most - counts[i], max(1, budget * loads[i] // mass), surplus)
            counts[i] = counts[i] + more
            surplus = surplus - more
    return np.array([most] + counts)


def ragged(stream_key, count, total, most, slope):
    if count == 2:
        one = jax.random.randint(stream_key, (), max(1, total - most), min(most, total - 1) + 1)
        return jnp.stack([one, total - one])
    sizes = jnp.asarray(length_profile(count, total, most, slope), jnp.int32)
    pairs = (count - 1) // 2
    donor, taker = sizes[1:1 + 2 * pairs:2], sizes[2:2 + 2 * pairs:2]
    room = jnp.minimum(donor - 1, most - taker)
    shifted = jax.random.randint(jax.random.fold_in(stream_key, 1), (pairs,), 0, 1 << 20) % (room + 1)
    sizes = sizes.at[1:1 + 2 * pairs:2].set(donor - shifted).at[2:2 + 2 * pairs:2].set(taker + shifted)
    return sizes[jax.random.permutation(jax.random.fold_in(stream_key, 2), count)]


def routed_block(own_key, own, number, rows, number_of, top, bound, slope):
    order = jax.random.permutation(own_key, number_of)
    heavy_load, usual = shares(number_of, rows * top, bound, slope, True), shares(number_of, rows * top, bound, slope, False)
    places = jnp.arange(number_of)

    def named(tallies, rotation):
        used = int((tallies > 0).sum())
        fixed = max(1, used // 4)
        passed = fixed + (places - fixed + rotation * (used - fixed)) % max(1, number_of - fixed)
        return jnp.zeros((number_of,), jnp.int32).at[order[jnp.where(places < fixed, places, passed)]].set(jnp.asarray(tallies, jnp.int32))

    tallies = jnp.where(number % 4 == 0, named(heavy_load, number // 4), named(usual, number - number // 4 - 1))
    mixed = jax.random.permutation(jax.random.fold_in(own, 3), number_of)
    source_of, taker = mixed[0:number_of // 2 * 2:2], mixed[1:number_of // 2 * 2:2]
    margin = jnp.minimum(tallies[source_of] - 1, bound - tallies[taker]) // 2
    margin = jnp.where((source_of == order[0]) | (taker == order[0]) | (tallies[taker] == 0), 0, jnp.maximum(margin, 0))
    passed = jax.random.randint(jax.random.fold_in(own, 4), (number_of // 2,), 0, 1 << 20) % (margin + 1)
    tallies = tallies.at[source_of].add(-passed).at[taker].add(passed)
    items = jnp.searchsorted(jnp.cumsum(tallies), jnp.arange(rows * top), side="right").astype(jnp.int32)
    grid = items.reshape(top, rows).T
    grid = grid[jax.random.permutation(jax.random.fold_in(own, 1), rows)]
    rotation = jax.random.randint(jax.random.fold_in(own, 2), (rows, 1), 0, top)
    return jnp.take_along_axis(grid, (jnp.arange(top)[None, :] + rotation) % top, axis=1)


def shares(number_of, total, most, skew, full):
    loads = [(1 << 20) // math.isqrt(grade ** skew) + 1 for grade in range(1, number_of + 1)]
    largest = most if full else min(most, max(-(-total // number_of), total * loads[0] // sum(loads)))
    least = 1 if total - largest >= number_of - 1 else 0
    holding, spare = [largest] + [least] * (number_of - 1), total - largest - least * (number_of - 1)
    while spare > 0:
        movable = [i for i in range(1, number_of) if holding[i] < largest] or [i for i in range(1, number_of) if holding[i] < most]
        mass, left = sum([loads[i] for i in movable]), spare
        for i in movable:
            addition = min(most - holding[i], max(1, left * loads[i] // mass), spare)
            holding[i] = holding[i] + addition
            spare = spare - addition
    return np.array(holding)


def bell_draw(stream_key, extent, deviation, most, pieces=(), kind=jnp.bfloat16):
    entries = deviation * jax.random.normal(stream_key, extent, jnp.float32)
    if pieces:
        entries = entries * level_of(stream_key, extent, pieces, -0.22, 0.18)
    return jnp.clip(entries, -most, most).astype(kind)


def setup_inputs(seed: int = 0) -> dict:
    key_of = jax.random.split(jax.random.key(seed), 9)
    hidden = draw_hidden(jax.random.fold_in(key_of[8], 71), 0)
    audio = draw_audio(jax.random.fold_in(key_of[8], 71), 0)
    audio_dest_keys = jax.random.split(jax.random.fold_in(key_of[2], 1), (N_SECTION * AUD_DEV) // AUD_DEV)
    audio_dest_turns = jax.random.permutation(jax.random.fold_in(key_of[2], 3), (N_SECTION * AUD_DEV) // AUD_DEV)
    audio_dest = jax.vmap(lambda own, number: routed_block(jax.random.fold_in(key_of[2], 2), own, number, AUD_DEV, N_SECTION, 1, CAP, 2))(audio_dest_keys, audio_dest_turns).reshape((N_SECTION * AUD_DEV, 1))
    segment = jax.vmap(lambda own: jnp.searchsorted(jnp.cumsum(ragged(own, 4, MB_ROWS, MB_ROWS // 2, 2)), jnp.arange(MB_ROWS), side="right"))(jax.random.split(key_of[3], (N_SECTION * MB_DEV))).reshape((N_SECTION * MB_DEV, MB_ROWS)).astype(jnp.int32)
    norm_gain = jnp.clip(1.0 + 0.15 * jax.random.normal(key_of[4], (N_SECTION, D), jnp.float32), 0.25, 1.75).astype(jnp.bfloat16)
    w_query = draw_w_query(jax.random.fold_in(key_of[8], 71), 0)
    w_keyval = draw_w_keyval(jax.random.fold_in(key_of[8], 71), 0)
    w_out = bell_draw(key_of[7], (N_SECTION, HEADS * HD, D), (HEADS * HD) ** -0.5, 0.09375, ((0, 16), (2, 32)))
    return {"hidden": hidden, "audio": audio, "audio_dest": audio_dest, "segment": segment, "norm_gain": norm_gain, "w_query": w_query, "w_keyval": w_keyval, "w_out": w_out}


def rotate(values, cosine, sine):
    half = values.shape[-1] // 2
    first = values[..., :half]
    second = values[..., half:]
    return jnp.concatenate([first * cosine - second * sine, second * cosine + first * sine], -1)

def rope_tables(rows, width):
    position = jnp.arange(rows, dtype=jnp.float32)
    freq = 500000.0 ** (-(2.0 * jnp.arange(width // 2, dtype=jnp.float32)) / width)
    angle = position[:, None] * freq[None, :]
    return (jnp.cos(angle), jnp.sin(angle))

def section_layer(state, gain, w_q, w_kv, w_o, segment_now, live_keys, cosine, sine):
    state_wide = state.astype(jnp.float32)
    inverse = lax.rsqrt(lax.optimization_barrier(jnp.mean(state_wide * state_wide, axis=1, keepdims=True)) + 1e-05)
    normed = (state_wide * inverse * gain.astype(jnp.float32)[None, :]).astype(jnp.bfloat16)
    queries = jnp.dot(normed, w_q, preferred_element_type=jnp.float32).reshape(MB_DEV, MB_ROWS, HEADS, HD)
    key_values = jnp.dot(normed, w_kv, preferred_element_type=jnp.float32).reshape(MB_DEV, MB_ROWS, KVH, 2, HD)
    key_rows = key_values[:, :, :, 0]
    value_rows = key_values[:, :, :, 1].astype(jnp.bfloat16)
    queries = rotate(queries, cosine[:, None, :], sine[:, None, :]).astype(jnp.bfloat16)
    key_rows = rotate(key_rows, cosine[:, None, :], sine[:, None, :]).astype(jnp.bfloat16)
    group = HEADS // KVH
    key_rows = jnp.repeat(key_rows, group, axis=2)
    value_rows = jnp.repeat(value_rows, group, axis=2)
    scores = jnp.einsum('mihd,mjhd->mhij', queries.astype(jnp.float32), key_rows.astype(jnp.float32)) * (1.0 / math.sqrt(HD))
    row_ids = jnp.arange(MB_ROWS, dtype=jnp.int32)
    causal = row_ids[None, :] <= row_ids[:, None]
    diagonal = row_ids[None, :] == row_ids[:, None]
    allowed = causal[None] & (segment_now[:, :, None] == segment_now[:, None, :]) & (live_keys[:, None, :] | diagonal[None])
    scores = jnp.where(allowed[:, None], scores, -jnp.inf)
    highest = lax.optimization_barrier(jnp.max(scores, axis=-1, keepdims=True))
    weights = jnp.exp(scores - highest)
    probs = (weights / lax.optimization_barrier(jnp.sum(weights, axis=-1, keepdims=True))).astype(jnp.bfloat16)
    attended = jnp.einsum('mhij,mjhd->mihd', probs.astype(jnp.float32), value_rows.astype(jnp.float32)).astype(jnp.bfloat16)
    attended = attended.reshape(MB_DEV * MB_ROWS, HEADS * HD)
    projected = jnp.dot(attended, w_o, preferred_element_type=jnp.float32)
    return (state_wide + projected).astype(jnp.bfloat16)

def reference(hidden, audio, audio_dest, segment, norm_gain, w_query, w_keyval, w_out):
    targets = audio_dest[:, 0].reshape(N_SECTION, AUD_DEV).astype(jnp.int32)
    order = jnp.arange(AUD_DEV, dtype=jnp.int32)
    earlier = order[None, :] < order[:, None]
    row_rank = lax.optimization_barrier(jnp.sum(((targets[:, :, None] == targets[:, None, :]) & earlier[None]).astype(jnp.int32), axis=2)).astype(jnp.int32)
    sources = jnp.broadcast_to(jnp.arange(N_SECTION, dtype=jnp.int32)[:, None], targets.shape)
    slot_index = (sources * CAP + row_rank).astype(jnp.int32)
    audio_slots = jnp.zeros((N_SECTION, MB_DEV * AUD_MB, D), jnp.bfloat16).at[targets, slot_index].set(audio.reshape(N_SECTION, AUD_DEV, D))
    live_audio = jnp.zeros((N_SECTION, MB_DEV * AUD_MB), jnp.bool_).at[targets, slot_index].set(True)
    text_rows = hidden.reshape(N_SECTION, MB_DEV, TXT_MB, D)
    state = jnp.concatenate([audio_slots.reshape(N_SECTION, MB_DEV, AUD_MB, D), text_rows], 2).reshape(N_SECTION, MB_DEV * MB_ROWS, D)
    live_keys = jnp.concatenate([live_audio.reshape(N_SECTION, MB_DEV, AUD_MB), jnp.ones((N_SECTION, MB_DEV, TXT_MB), jnp.bool_)], 2)
    segment_now = segment.reshape(N_SECTION, MB_DEV, MB_ROWS)
    cosine, sine = rope_tables(MB_ROWS, HD)

    def one_stop(packed):
        return section_layer(packed[0], packed[1], packed[2], packed[3], packed[4], packed[5], packed[6], cosine, sine)
    for lap_step in range(STEPS):
        state = lax.map(one_stop, (state, norm_gain, w_query, w_keyval, w_out, segment_now, live_keys))
        state = jnp.roll(state, 1, 0)
        segment_now = jnp.roll(segment_now, 1, 0)
        live_keys = jnp.roll(live_keys, 1, 0)
    return state.reshape(N_SECTION * MB_DEV * MB_ROWS, D)
```

```python
import math

import jax
import jax.numpy as jnp
from jax import lax
from jax.sharding import Mesh
from jax.sharding import PartitionSpec as P

D = 8192
HD = 128
KVH = 4
MB_DEV = 2
AUD_MB = 32
TXT_MB = 32
AUD_DEV = 32
STEPS = 4
MB_ROWS = 64
CAP = 4
COLS = 256
GROUP = 4
F32 = jnp.float32
BF16 = jnp.bfloat16


def shift(block, axis, distance):
    count = lax.axis_size(axis)
    return lax.ppermute(block, axis, [(i, (i + distance) % count) for i in range(count)])


def rotate(values, cosine, sine):
    half = values.shape[-1] // 2
    first = values[..., :half]
    second = values[..., half:]
    return jnp.concatenate([first * cosine - second * sine, second * cosine + first * sine], -1)


def rope_tables(rows, width):
    position = jnp.arange(rows, dtype=F32)
    freq = 500000.0 ** (-(2.0 * jnp.arange(width // 2, dtype=F32)) / width)
    angle = position[:, None] * freq[None, :]
    return (jnp.cos(angle), jnp.sin(angle))


def pick(stack, index, axis):
    return lax.dynamic_index_in_dim(stack, index, axis, keepdims=False)


def in_order(own, other, y, axis):
    first = jnp.where(y == 0, own, other)
    second = jnp.where(y == 0, other, own)
    return jnp.concatenate([first, second], axis)


def local(hidden, audio, audio_dest, segment, norm_gain, w_query, w_keyval, w_out):
    stops = lax.axis_size("section")
    s = lax.axis_index("section")
    a = lax.axis_index("za")
    b = lax.axis_index("zb")
    y = lax.axis_index("y")

    w_q = w_query[0].reshape(GROUP, GROUP, 2 * COLS, HD)
    query_parts = []
    for j in range(GROUP):
        piece = pick(w_q, (b - j) % GROUP, 1)
        if j:
            piece = shift(piece, "zb", -j)
        piece = piece.reshape(GROUP * 2 * COLS, HD)
        query_parts.append(jnp.concatenate([piece, shift(piece, "y", 1)], 1))

    w_kv = w_keyval[0].reshape(COLS, GROUP, 2 * HD)
    kv_pieces = []
    for k in range(GROUP):
        piece = pick(w_kv, (a + k) % GROUP, 1)
        if k:
            piece = shift(piece, "za", k)
        kv_pieces.append(piece)
    kv_stack = jnp.stack(kv_pieces)
    kv_own = jnp.stack([pick(kv_stack, (a - source) % GROUP, 0) for source in range(GROUP)])
    kv_other = shift(kv_own, "y", 1)
    w_kv_rows = in_order(kv_own, kv_other, y, 1).reshape(GROUP * 2 * COLS, 2 * HD)

    w_o = w_out[0]
    w_o_pair = jnp.concatenate([w_o, shift(w_o, "y", 1)], 1)

    targets = audio_dest[:, 0].reshape(stops, AUD_DEV)
    order = jnp.arange(AUD_DEV, dtype=jnp.int32)
    own_targets = pick(targets, s, 0)
    rank = jnp.sum(
        ((own_targets[:, None] == own_targets[None, :]) & (order[None, :] < order[:, None])).astype(jnp.int32),
        axis=1,
    )
    seats = jnp.arange(stops * CAP, dtype=jnp.int32)
    chosen = seats[:, None] == (own_targets * CAP + rank)[None, :]
    outgoing = jnp.dot(chosen.astype(BF16), audio, preferred_element_type=F32).astype(BF16)
    slots = lax.all_to_all(outgoing.reshape(stops, CAP, COLS), "section", 0, 0, tiled=True)
    slots = slots.reshape(MB_DEV, AUD_MB, COLS)
    text = hidden.reshape(MB_DEV, TXT_MB, COLS)
    gain_rows = jnp.broadcast_to(norm_gain, (16, COLS))

    def batch(index):
        return jnp.concatenate([pick(slots, index, 0), pick(text, index, 0), gain_rows], 0)

    both = in_order(batch(y), shift(batch(1 - y), "y", 1), y, 1)
    state = both[:MB_ROWS]
    gain = None

    seat_ids = jnp.arange(AUD_MB, dtype=jnp.int32)
    owner = y * (AUD_MB // CAP) + seat_ids // CAP
    row_ids = jnp.arange(MB_ROWS, dtype=jnp.int32)
    causal = row_ids[None, :] <= row_ids[:, None]
    diagonal = row_ids[None, :] == row_ids[:, None]
    allowed = []
    for lap_step in range(STEPS):
        root = (s - lap_step) % stops
        clip = pick(segment, root * MB_DEV + y, 0)
        counts = jnp.sum((targets == root).astype(jnp.int32), axis=1)
        held = jnp.sum(
            jnp.where(owner[:, None] == jnp.arange(stops, dtype=jnp.int32)[None, :], counts[None, :], 0), axis=1
        )
        live = jnp.concatenate([seat_ids % CAP < held, jnp.ones((TXT_MB,), jnp.bool_)], 0)
        allowed.append(causal & (clip[:, None] == clip[None, :]) & (live[None, :] | diagonal))
    cosine, sine = rope_tables(MB_ROWS, HD)
    scale = 1.0 / math.sqrt(HD)
    lane = jnp.arange(HD, dtype=jnp.int32)[None, :]

    for lap_step in range(STEPS):
        if lap_step == 0:
            wide = lax.all_gather(both, "za", axis=1, tiled=True)
            gain = wide[MB_ROWS : MB_ROWS + 1].astype(F32)
            wide = wide[:MB_ROWS]
        else:
            wide = lax.all_gather(state, "za", axis=1, tiled=True)
        wide = wide.astype(F32)
        squares = jnp.sum(wide * wide, axis=1, keepdims=True)
        scaled = (wide * gain).astype(BF16)
        queries = [jnp.dot(scaled, part, preferred_element_type=F32).astype(BF16) for part in query_parts]
        key_values = jnp.dot(scaled, w_kv_rows, preferred_element_type=F32).astype(BF16)
        coarse = squares.astype(BF16)
        middle = (squares - coarse.astype(F32)).astype(BF16)
        fine = (squares - coarse.astype(F32) - middle.astype(F32)).astype(BF16)
        square_lanes = jnp.where(
            lane == 0, coarse, jnp.where(lane == 1, middle, jnp.where(lane == 2, fine, jnp.zeros((), BF16)))
        )
        by_receiver = lax.dynamic_slice_in_dim(jnp.stack(queries + queries), (GROUP - b) % GROUP, GROUP, 0)
        shared = jnp.concatenate([key_values, square_lanes], 1)
        message = jnp.concatenate([by_receiver, jnp.broadcast_to(shared[None], (GROUP,) + shared.shape)], 2)
        arrived = lax.all_to_all(message, "zb", 0, 0, tiled=True)
        total = jnp.sum(arrived.astype(F32), axis=0)
        inverse = lax.rsqrt(jnp.sum(total[:, 4 * HD :], axis=1, keepdims=True) / D + 1e-05)
        total = total[:, : 4 * HD] * inverse
        key_rows = rotate(total[:, 2 * HD : 3 * HD], cosine, sine).astype(BF16)
        value_rows = total[:, 3 * HD :].astype(BF16)
        heads = []
        for head in range(2):
            query_rows = rotate(total[:, head * HD : (head + 1) * HD], cosine, sine).astype(BF16)
            scores = jnp.dot(query_rows, key_rows.T, preferred_element_type=F32) * scale
            scores = jnp.where(allowed[lap_step], scores, -jnp.inf)
            weights = jnp.exp(scores - jnp.max(scores, axis=-1, keepdims=True))
            probs = (weights / jnp.sum(weights, axis=-1, keepdims=True)).astype(BF16)
            heads.append(jnp.dot(probs, value_rows, preferred_element_type=F32).astype(BF16))
        attended = lax.all_gather(in_order(heads[0], heads[1], y, 1), ("za", "zb"), axis=1, tiled=True)
        projected = jnp.dot(attended, w_o_pair, preferred_element_type=F32)
        state_wide = state.astype(F32)
        if lap_step < STEPS - 1:
            update = in_order(projected[:, :COLS], projected[:, COLS:], y, 1)
            state = shift((state_wide + update).astype(BF16), "section", 1)
    low, high = state_wide[:, :COLS], state_wide[:, COLS:]
    own = (jnp.where(y == 0, low, high) + projected[:, :COLS]).astype(BF16)
    other = (jnp.where(y == 0, high, low) + projected[:, COLS:]).astype(BF16)
    crossing = [(2 * i + j, 2 * ((i + 1) % stops) + 1 - j) for i in range(stops) for j in range(2)]
    own = shift(own, "section", 1)
    other = lax.ppermute(other, ("section", "y"), crossing)
    return in_order(own, other, y, 0)


def solution(mesh):
    sections = mesh.shape["section"]
    parts = mesh.shape["tensor"]
    names = ("section", "za", "zb", "y")
    fine = Mesh(mesh.devices.reshape(sections, parts // (2 * GROUP), GROUP, 2), names)
    tensor = names[1:]
    in_specs = (
        P("section", tensor),
        P("section", tensor),
        P(),
        P(),
        P("section", tensor),
        P("section", None, tensor),
        P("section", tensor, None),
        P("section", None, tensor),
    )
    return jax.shard_map(local, mesh=fine, in_specs=in_specs, out_specs=P("section", tensor), check_vma=False)
```

```python
import math

import jax
import jax.numpy as jnp
from jax import lax
from jax.sharding import Mesh
from jax.sharding import PartitionSpec as P

D = 8192
HD = 128
KVH = 4
MB_DEV = 2
AUD_MB = 32
TXT_MB = 32
AUD_DEV = 32
STEPS = 4
MB_ROWS = 64
CAP = 4
COLS = 256
GROUP = 4
F32 = jnp.float32
BF16 = jnp.bfloat16


def shift(block, axis, distance):
    count = lax.axis_size(axis)
    return lax.ppermute(block, axis, [(i, (i + distance) % count) for i in range(count)])


def rotate(values, cosine, sine):
    half = values.shape[-1] // 2
    first = values[..., :half]
    second = values[..., half:]
    return jnp.concatenate([first * cosine - second * sine, second * cosine + first * sine], -1)


def rope_tables(rows, width):
    position = jnp.arange(rows, dtype=F32)
    freq = 500000.0 ** (-(2.0 * jnp.arange(width // 2, dtype=F32)) / width)
    angle = position[:, None] * freq[None, :]
    return (jnp.cos(angle), jnp.sin(angle))


def pick(stack, index, axis):
    return lax.dynamic_index_in_dim(stack, index, axis, keepdims=False)


def to_all(block, count):
    return jnp.broadcast_to(block[None], (count,) + block.shape)


def split_float(values):
    coarse = values.astype(BF16)
    rest = values - coarse.astype(F32)
    middle = rest.astype(BF16)
    lane = jnp.arange(HD, dtype=jnp.int32)[None, :]
    fine = (rest - middle.astype(F32)).astype(BF16)
    zero = jnp.zeros((), BF16)
    return jnp.where(lane == 0, coarse, jnp.where(lane == 1, middle, jnp.where(lane == 2, fine, zero)))


def in_order(own, other, y, axis):
    first = jnp.where(y == 0, own, other)
    second = jnp.where(y == 0, other, own)
    return jnp.concatenate([first, second], axis)


def local(hidden, audio, audio_dest, segment, norm_gain, w_query, w_keyval, w_out):
    stops = lax.axis_size("section")
    s = lax.axis_index("section")
    a = lax.axis_index("za")
    b = lax.axis_index("zb")
    y = lax.axis_index("y")

    targets = audio_dest[:, 0].reshape(stops, AUD_DEV)
    half_stops = stops // MB_DEV

    order = jnp.arange(AUD_DEV, dtype=jnp.int32)
    own_targets = pick(targets, s, 0)
    rank = jnp.sum(
        ((own_targets[:, None] == own_targets[None, :]) & (order[None, :] < order[:, None])).astype(jnp.int32),
        axis=1,
    )
    holder = 2 * own_targets + s // half_stops
    seats = jnp.arange(stops * MB_DEV * CAP, dtype=jnp.int32)
    chosen = seats[:, None] == (holder * CAP + rank)[None, :]
    outgoing = jnp.dot(chosen.astype(BF16), audio, preferred_element_type=F32).astype(BF16)
    outgoing, w_keys, w_queries = lax.optimization_barrier((outgoing, w_keyval[0], w_query[0]))
    slots = lax.all_to_all(outgoing.reshape(stops * MB_DEV, CAP, COLS), ("section", "y"), 0, 0, tiled=True)
    slots = pick(slots.reshape(MB_DEV, half_stops, 2, CAP, COLS), y, 0)
    slots = slots.transpose(0, 2, 1, 3).reshape(AUD_MB, 2 * COLS)

    text = hidden.reshape(MB_DEV, TXT_MB, COLS)
    gain_rows = jnp.broadcast_to(norm_gain, (16, COLS))

    def batch(index):
        return jnp.concatenate([pick(text, index, 0), gain_rows], 0)

    written = in_order(batch(y), shift(batch(1 - y), "y", 1), y, 1)
    features = GROUP * 2 * COLS
    w_kv = w_keys.reshape(COLS, GROUP, 2 * HD)
    kv_pieces = [pick(w_kv, (a + k) % GROUP, 1) for k in range(GROUP)]
    kv_stack = jnp.stack([shift(piece, "za", k) if k else piece for k, piece in enumerate(kv_pieces)])
    kv_own = jnp.stack([pick(kv_stack, (a - source) % GROUP, 0) for source in range(GROUP)])
    both, kv_own = lax.optimization_barrier((jnp.concatenate([slots, written], 0), kv_own))
    state = both[:MB_ROWS]
    w_kv_rows = in_order(kv_own, shift(kv_own, "y", 1), y, 1).reshape(features, 2 * HD)
    w_q = w_queries.reshape(GROUP, GROUP, 2 * COLS, HD)
    rows_own = jnp.stack([pick(w_q, (b - j) % GROUP, 1).reshape(features, HD) for j in range(GROUP)])
    rows_other = shift(rows_own, "y", 1)

    seat_ids = jnp.arange(AUD_MB, dtype=jnp.int32)
    owner = y * (AUD_MB // CAP) + seat_ids // CAP
    row_ids = jnp.arange(MB_ROWS, dtype=jnp.int32)
    causal = row_ids[None, :] <= row_ids[:, None]
    diagonal = row_ids[None, :] == row_ids[:, None]
    allowed = []
    for lap_step in range(STEPS):
        root = (s - lap_step) % stops
        clip = pick(segment, root * MB_DEV + y, 0)
        counts = jnp.sum((targets == root).astype(jnp.int32), axis=1)
        held = jnp.sum(
            jnp.where(owner[:, None] == jnp.arange(stops, dtype=jnp.int32)[None, :], counts[None, :], 0), axis=1
        )
        live = jnp.concatenate([seat_ids % CAP < held, jnp.ones((TXT_MB,), jnp.bool_)], 0)
        allowed.append(causal & (clip[:, None] == clip[None, :]) & (live[None, :] | diagonal))
    cosine, sine = rope_tables(MB_ROWS, HD)
    scale = 1.0 / math.sqrt(HD)

    for lap_step in range(STEPS):
        if lap_step == 0:
            wide = lax.all_gather(both, "za", axis=1, tiled=True)
            wide, w_o = lax.optimization_barrier((wide, w_out[0]))
            w_o_halves = (w_out[0], shift(w_o, "y", 1))
            w_pair = lax.optimization_barrier(jnp.concatenate([rows_own, rows_other], 2))
            gain_wide = wide[MB_ROWS : MB_ROWS + 1].astype(F32)
            wide = wide[:MB_ROWS].astype(F32)
        else:
            wide = lax.all_gather(state, "za", axis=1, tiled=True).astype(F32)
        scaled = (wide * gain_wide).astype(BF16)
        squares = jnp.sum(wide * wide, axis=1, keepdims=True)
        key_values = jnp.dot(scaled, w_kv_rows, preferred_element_type=F32).astype(BF16)
        payload = jnp.concatenate([scaled, key_values, split_float(squares)], 1)
        gathered = [payload] + [shift(payload, "zb", j) for j in range(1, GROUP)]
        total = sum(part[:, features:].astype(F32) for part in gathered)
        queries = sum(
            jnp.dot(part[:, :features], w_pair[j], preferred_element_type=F32) for j, part in enumerate(gathered)
        )
        total = jnp.concatenate([queries, total], 1)
        inverse = lax.rsqrt(jnp.sum(total[:, 4 * HD :], axis=1, keepdims=True) / D + 1e-05)
        total = total[:, : 4 * HD] * inverse
        key_rows = rotate(total[:, 2 * HD : 3 * HD], cosine, sine).astype(BF16)
        value_rows = total[:, 3 * HD :].astype(BF16)
        heads = []
        for head in range(2):
            query_rows = rotate(total[:, head * HD : (head + 1) * HD], cosine, sine).astype(BF16)
            scores = jnp.dot(query_rows, key_rows.T, preferred_element_type=F32) * scale
            scores = jnp.where(allowed[lap_step], scores, -jnp.inf)
            weights = jnp.exp(scores - jnp.max(scores, axis=-1, keepdims=True))
            probs = (weights / jnp.sum(weights, axis=-1, keepdims=True)).astype(BF16)
            heads.append(jnp.dot(probs, value_rows, preferred_element_type=F32).astype(BF16))
        attended = in_order(heads[0], heads[1], y, 1)
        attended = lax.all_gather(attended, ("za", "zb"), axis=1, tiled=True)
        projected = [jnp.dot(attended, half, preferred_element_type=F32) for half in w_o_halves]
        state_wide = state.astype(F32)
        if lap_step < STEPS - 1:
            update = in_order(projected[0], projected[1], y, 1)
            state = shift((state_wide + update).astype(BF16), "section", 1)
    low, high = state_wide[:, :COLS], state_wide[:, COLS:]
    own = (jnp.where(y == 0, low, high) + projected[0]).astype(BF16)
    other = (jnp.where(y == 0, high, low) + projected[1]).astype(BF16)
    crossing = [(2 * i + j, 2 * ((i + 1) % stops) + 1 - j) for i in range(stops) for j in range(2)]
    own = shift(own, "section", 1)
    other = lax.ppermute(other, ("section", "y"), crossing)
    return in_order(own, other, y, 0)


def solution(mesh):
    sections = mesh.shape["section"]
    parts = mesh.shape["tensor"]
    names = ("section", "za", "zb", "y")
    fine = Mesh(mesh.devices.reshape(sections, parts // (2 * GROUP), GROUP, 2), names)
    tensor = names[1:]
    in_specs = (
        P("section", tensor),
        P("section", tensor),
        P(),
        P(),
        P("section", tensor),
        P("section", None, tensor),
        P("section", tensor, None),
        P("section", None, tensor),
    )
    return jax.shard_map(local, mesh=fine, in_specs=in_specs, out_specs=P("section", tensor), check_vma=False)
```

```python
import math

import jax
import jax.numpy as jnp
from jax import lax
from jax.sharding import Mesh
from jax.sharding import PartitionSpec as P

D = 8192
HD = 128
KVH = 4
MB_DEV = 2
AUD_MB = 32
TXT_MB = 32
AUD_DEV = 32
STEPS = 4
MB_ROWS = 64
CAP = 4
COLS = 256
GROUP = 4
F32 = jnp.float32
BF16 = jnp.bfloat16


def shift(block, axis, distance):
    count = lax.axis_size(axis)
    return lax.ppermute(block, axis, [(i, (i + distance) % count) for i in range(count)])


def rotate(values, cosine, sine):
    half = values.shape[-1] // 2
    first = values[..., :half]
    second = values[..., half:]
    return jnp.concatenate([first * cosine - second * sine, second * cosine + first * sine], -1)


def rope_tables(rows, width):
    position = jnp.arange(rows, dtype=F32)
    freq = 500000.0 ** (-(2.0 * jnp.arange(width // 2, dtype=F32)) / width)
    angle = position[:, None] * freq[None, :]
    return (jnp.cos(angle), jnp.sin(angle))


def pick(stack, index, axis):
    return lax.dynamic_index_in_dim(stack, index, axis, keepdims=False)


def to_all(block, count):
    return jnp.broadcast_to(block[None], (count,) + block.shape)


def split_float(values):
    coarse = values.astype(BF16)
    rest = values - coarse.astype(F32)
    middle = rest.astype(BF16)
    lane = jnp.arange(HD, dtype=jnp.int32)[None, :]
    fine = (rest - middle.astype(F32)).astype(BF16)
    zero = jnp.zeros((), BF16)
    return jnp.where(lane == 0, coarse, jnp.where(lane == 1, middle, jnp.where(lane == 2, fine, zero)))


def in_order(own, other, y, axis):
    first = jnp.where(y == 0, own, other)
    second = jnp.where(y == 0, other, own)
    return jnp.concatenate([first, second], axis)


def local(hidden, audio, audio_dest, segment, norm_gain, w_query, w_keyval, w_out):
    stops = lax.axis_size("section")
    s = lax.axis_index("section")
    a = lax.axis_index("za")
    b = lax.axis_index("zb")
    y = lax.axis_index("y")

    features = GROUP * 2 * COLS
    w_q = w_query[0].reshape(GROUP, GROUP, 2 * COLS, HD)
    parts = [pick(w_q, (b - j) % GROUP, 1).reshape(features, HD) for j in range(GROUP)]
    group_own = [shift(part, "zb", -j) if j else part for j, part in enumerate(parts)]

    text = hidden.reshape(MB_DEV, TXT_MB, COLS)
    gain_rows = jnp.broadcast_to(norm_gain, (16, COLS))

    def batch(index):
        return jnp.concatenate([pick(text, index, 0), gain_rows], 0)

    written = in_order(batch(y), shift(batch(1 - y), "y", 1), y, 1)
    targets = audio_dest[:, 0].reshape(stops, AUD_DEV)
    half_stops = stops // MB_DEV

    order = jnp.arange(AUD_DEV, dtype=jnp.int32)
    own_targets = pick(targets, s, 0)
    rank = jnp.sum(
        ((own_targets[:, None] == own_targets[None, :]) & (order[None, :] < order[:, None])).astype(jnp.int32),
        axis=1,
    )
    holder = 2 * own_targets + s // half_stops
    seats = jnp.arange(stops * MB_DEV * CAP, dtype=jnp.int32)
    chosen = seats[:, None] == (holder * CAP + rank)[None, :]
    outgoing = jnp.dot(chosen.astype(BF16), audio, preferred_element_type=F32).astype(BF16)
    slots = lax.all_to_all(outgoing.reshape(stops * MB_DEV, CAP, COLS), ("section", "y"), 0, 0, tiled=True)
    slots = pick(slots.reshape(MB_DEV, half_stops, 2, CAP, COLS), y, 0)
    slots = slots.transpose(0, 2, 1, 3).reshape(AUD_MB, 2 * COLS)

    both = jnp.concatenate([slots, written], 0)
    first_other = shift(parts[0], "y", 1)
    both, group_own, first_other, w_kv = lax.optimization_barrier((both, group_own, first_other, w_keyval[0]))
    state = both[:MB_ROWS]
    group_other = shift(jnp.stack(group_own[1:]), "y", 1)
    w_kv = w_kv.reshape(COLS, GROUP, 2 * HD).transpose(1, 0, 2)
    kv_own = lax.all_to_all(w_kv, "za", 0, 0, tiled=True)
    both, kv_own = lax.optimization_barrier((both, kv_own))
    w_kv_rows = in_order(kv_own, shift(kv_own, "y", 1), y, 1).reshape(features, 2 * HD)
    group_other = [first_other] + [group_other[j] for j in range(GROUP - 1)]
    w_group = [jnp.concatenate([mine, others], 1) for mine, others in zip(group_own, group_other)]
    w_group = lax.optimization_barrier(w_group)

    seat_ids = jnp.arange(AUD_MB, dtype=jnp.int32)
    owner = y * (AUD_MB // CAP) + seat_ids // CAP
    row_ids = jnp.arange(MB_ROWS, dtype=jnp.int32)
    causal = row_ids[None, :] <= row_ids[:, None]
    diagonal = row_ids[None, :] == row_ids[:, None]
    allowed = []
    for lap_step in range(STEPS):
        root = (s - lap_step) % stops
        clip = pick(segment, root * MB_DEV + y, 0)
        counts = jnp.sum((targets == root).astype(jnp.int32), axis=1)
        held = jnp.sum(
            jnp.where(owner[:, None] == jnp.arange(stops, dtype=jnp.int32)[None, :], counts[None, :], 0), axis=1
        )
        live = jnp.concatenate([seat_ids % CAP < held, jnp.ones((TXT_MB,), jnp.bool_)], 0)
        allowed.append(causal & (clip[:, None] == clip[None, :]) & (live[None, :] | diagonal))
    cosine, sine = rope_tables(MB_ROWS, HD)
    scale = 1.0 / math.sqrt(HD)

    for lap_step in range(STEPS):
        if lap_step == 0:
            wide = lax.all_gather(both, "za", axis=1, tiled=True)
            wide, w_o = lax.optimization_barrier((wide, w_out[0]))
            w_o_pair = lax.optimization_barrier(jnp.concatenate([w_out[0], shift(w_o, "y", 1)], 1))
            gain_wide = wide[MB_ROWS : MB_ROWS + 1].astype(F32)
            wide = wide[:MB_ROWS].astype(F32)
        else:
            wide = lax.all_gather(state, "za", axis=1, tiled=True).astype(F32)
        scaled = (wide * gain_wide).astype(BF16)
        squares = jnp.sum(wide * wide, axis=1, keepdims=True)
        queries = [jnp.dot(scaled, part, preferred_element_type=F32).astype(BF16) for part in w_group]
        key_values = jnp.dot(scaled, w_kv_rows, preferred_element_type=F32).astype(BF16)
        shared = jnp.concatenate([key_values, split_float(squares)], 1)
        message = jnp.stack([jnp.concatenate([part, shared], 1) for part in queries])
        message = jnp.roll(message, b, axis=0)
        arrived = lax.all_to_all(message, "zb", 0, 0, tiled=True)
        total = jnp.sum(arrived.astype(F32), axis=0)
        inverse = lax.rsqrt(jnp.sum(total[:, 4 * HD :], axis=1, keepdims=True) / D + 1e-05)
        total = total[:, : 4 * HD] * inverse
        key_rows = rotate(total[:, 2 * HD : 3 * HD], cosine, sine).astype(BF16)
        value_rows = total[:, 3 * HD :].astype(BF16)
        heads = []
        for head in range(2):
            query_rows = rotate(total[:, head * HD : (head + 1) * HD], cosine, sine).astype(BF16)
            scores = jnp.dot(query_rows, key_rows.T, preferred_element_type=F32) * scale
            scores = jnp.where(allowed[lap_step], scores, -jnp.inf)
            weights = jnp.exp(scores - jnp.max(scores, axis=-1, keepdims=True))
            probs = (weights / jnp.sum(weights, axis=-1, keepdims=True)).astype(BF16)
            heads.append(jnp.dot(probs, value_rows, preferred_element_type=F32).astype(BF16))
        attended = in_order(heads[0], heads[1], y, 1)
        if lap_step in (1, 2):
            attended = lax.all_to_all(to_all(attended, GROUP * GROUP), ("za", "zb"), 0, 0, tiled=True)
            attended = attended.transpose(1, 0, 2).reshape(MB_ROWS, GROUP * GROUP * 2 * HD)
        else:
            attended = lax.all_gather(attended, ("za", "zb"), axis=1, tiled=True)
        projected = jnp.dot(attended, w_o_pair, preferred_element_type=F32)
        state_wide = state.astype(F32)
        if lap_step < STEPS - 1:
            update = in_order(projected[:, :COLS], projected[:, COLS:], y, 1)
            state = shift((state_wide + update).astype(BF16), "section", 1)
    low, high = state_wide[:, :COLS], state_wide[:, COLS:]
    own = (jnp.where(y == 0, low, high) + projected[:, :COLS]).astype(BF16)
    other = (jnp.where(y == 0, high, low) + projected[:, COLS:]).astype(BF16)
    crossing = [(2 * i + j, 2 * ((i + 1) % stops) + 1 - j) for i in range(stops) for j in range(2)]
    own = shift(own, "section", 1)
    other = lax.ppermute(other, ("section", "y"), crossing)
    return in_order(own, other, y, 0)


def solution(mesh):
    sections = mesh.shape["section"]
    parts = mesh.shape["tensor"]
    names = ("section", "za", "zb", "y")
    fine = Mesh(mesh.devices.reshape(sections, parts // (2 * GROUP), GROUP, 2), names)
    tensor = names[1:]
    in_specs = (
        P("section", tensor),
        P("section", tensor),
        P(),
        P(),
        P("section", tensor),
        P("section", None, tensor),
        P("section", tensor, None),
        P("section", None, tensor),
    )
    return jax.shard_map(local, mesh=fine, in_specs=in_specs, out_specs=P("section", tensor), check_vma=False)
```

```python
import math

import jax
import jax.numpy as jnp
from jax import lax
from jax.sharding import Mesh
from jax.sharding import PartitionSpec as P

D = 8192
HD = 128
KVH = 4
MB_DEV = 2
AUD_MB = 32
TXT_MB = 32
AUD_DEV = 32
STEPS = 4
MB_ROWS = 64
CAP = 4
COLS = 256
GROUP = 4
F32 = jnp.float32
BF16 = jnp.bfloat16


def shift(block, axis, distance):
    count = lax.axis_size(axis)
    return lax.ppermute(block, axis, [(i, (i + distance) % count) for i in range(count)])


def rotate(values, cosine, sine):
    half = values.shape[-1] // 2
    first = values[..., :half]
    second = values[..., half:]
    return jnp.concatenate([first * cosine - second * sine, second * cosine + first * sine], -1)


def rope_tables(rows, width):
    position = jnp.arange(rows, dtype=F32)
    freq = 500000.0 ** (-(2.0 * jnp.arange(width // 2, dtype=F32)) / width)
    angle = position[:, None] * freq[None, :]
    return (jnp.cos(angle), jnp.sin(angle))


def pick(stack, index, axis):
    return lax.dynamic_index_in_dim(stack, index, axis, keepdims=False)


def to_all(block, count):
    return jnp.broadcast_to(block[None], (count,) + block.shape)


def split_float(values):
    coarse = values.astype(BF16)
    rest = values - coarse.astype(F32)
    middle = rest.astype(BF16)
    lane = jnp.arange(HD, dtype=jnp.int32)[None, :]
    fine = (rest - middle.astype(F32)).astype(BF16)
    zero = jnp.zeros((), BF16)
    return jnp.where(lane == 0, coarse, jnp.where(lane == 1, middle, jnp.where(lane == 2, fine, zero)))


def in_order(own, other, y, axis):
    first = jnp.where(y == 0, own, other)
    second = jnp.where(y == 0, other, own)
    return jnp.concatenate([first, second], axis)


def local(hidden, audio, audio_dest, segment, norm_gain, w_query, w_keyval, w_out):
    stops = lax.axis_size("section")
    s = lax.axis_index("section")
    a = lax.axis_index("za")
    b = lax.axis_index("zb")
    y = lax.axis_index("y")

    features = GROUP * 2 * COLS
    w_q = w_query[0].reshape(GROUP, GROUP, 2 * COLS, HD)
    parts = [pick(w_q, (b - j) % GROUP, 1).reshape(features, HD) for j in range(GROUP)]
    group_own = [shift(part, "zb", -j) if j else part for j, part in enumerate(parts)]

    text = hidden.reshape(MB_DEV, TXT_MB, COLS)
    gain_rows = jnp.broadcast_to(norm_gain, (16, COLS))

    def batch(index):
        return jnp.concatenate([pick(text, index, 0), gain_rows], 0)

    written = in_order(batch(y), shift(batch(1 - y), "y", 1), y, 1)
    targets = audio_dest[:, 0].reshape(stops, AUD_DEV)
    half_stops = stops // MB_DEV

    order = jnp.arange(AUD_DEV, dtype=jnp.int32)
    own_targets = pick(targets, s, 0)
    rank = jnp.sum(
        ((own_targets[:, None] == own_targets[None, :]) & (order[None, :] < order[:, None])).astype(jnp.int32),
        axis=1,
    )
    holder = 2 * own_targets + s // half_stops
    seats = jnp.arange(stops * MB_DEV * CAP, dtype=jnp.int32)
    chosen = seats[:, None] == (holder * CAP + rank)[None, :]
    outgoing = jnp.dot(chosen.astype(BF16), audio, preferred_element_type=F32).astype(BF16)
    slots = lax.all_to_all(outgoing.reshape(stops * MB_DEV, CAP, COLS), ("section", "y"), 0, 0, tiled=True)
    slots = pick(slots.reshape(MB_DEV, half_stops, 2, CAP, COLS), y, 0)
    slots = slots.transpose(0, 2, 1, 3).reshape(AUD_MB, 2 * COLS)

    both = jnp.concatenate([slots, written], 0)
    first_other = shift(parts[0], "y", 1)
    both, group_own, first_other, w_kv = lax.optimization_barrier((both, group_own, first_other, w_keyval[0]))
    state = both[:MB_ROWS]
    group_other = shift(jnp.stack(group_own[1:3]), "y", 1)
    w_kv = w_kv.reshape(COLS, GROUP, 2 * HD).transpose(1, 0, 2)
    kv_own = lax.all_to_all(w_kv, "za", 0, 0, tiled=True)
    both, kv_own = lax.optimization_barrier((both, kv_own))
    kv_flat = kv_own.reshape(GROUP * COLS, 2 * HD)
    kv_flat = jnp.concatenate([kv_flat[:, :HD], kv_flat[:, HD:]], 0)
    last = shift(jnp.stack([group_own[3], kv_flat]), "y", 1)
    kv_other = jnp.concatenate([last[1, : GROUP * COLS], last[1, GROUP * COLS :]], 1).reshape(kv_own.shape)
    w_kv_rows = in_order(kv_own, kv_other, y, 1).reshape(features, 2 * HD)
    group_other = [first_other, group_other[0], group_other[1], last[0]]
    w_group = [jnp.concatenate([mine, others], 1) for mine, others in zip(group_own, group_other)]
    w_group = lax.optimization_barrier(w_group)

    seat_ids = jnp.arange(AUD_MB, dtype=jnp.int32)
    owner = y * (AUD_MB // CAP) + seat_ids // CAP
    row_ids = jnp.arange(MB_ROWS, dtype=jnp.int32)
    causal = row_ids[None, :] <= row_ids[:, None]
    diagonal = row_ids[None, :] == row_ids[:, None]
    allowed = []
    for lap_step in range(STEPS):
        root = (s - lap_step) % stops
        clip = pick(segment, root * MB_DEV + y, 0)
        counts = jnp.sum((targets == root).astype(jnp.int32), axis=1)
        held = jnp.sum(
            jnp.where(owner[:, None] == jnp.arange(stops, dtype=jnp.int32)[None, :], counts[None, :], 0), axis=1
        )
        live = jnp.concatenate([seat_ids % CAP < held, jnp.ones((TXT_MB,), jnp.bool_)], 0)
        allowed.append(causal & (clip[:, None] == clip[None, :]) & (live[None, :] | diagonal))
    cosine, sine = rope_tables(MB_ROWS, HD)
    scale = 1.0 / math.sqrt(HD)

    for lap_step in range(STEPS):
        if lap_step == 0:
            wide = lax.all_gather(both, "za", axis=1, tiled=True)
            wide, w_o = lax.optimization_barrier((wide, w_out[0]))
            w_o_pair = lax.optimization_barrier(jnp.concatenate([w_out[0], shift(w_o, "y", 1)], 1))
            gain_wide = wide[MB_ROWS : MB_ROWS + 1].astype(F32)
            wide = wide[:MB_ROWS].astype(F32)
        else:
            wide = lax.all_gather(state, "za", axis=1, tiled=True).astype(F32)
        scaled = (wide * gain_wide).astype(BF16)
        squares = jnp.sum(wide * wide, axis=1, keepdims=True)
        queries = [jnp.dot(scaled, part, preferred_element_type=F32).astype(BF16) for part in w_group]
        key_values = jnp.dot(scaled, w_kv_rows, preferred_element_type=F32).astype(BF16)
        shared = jnp.concatenate([key_values, split_float(squares)], 1)
        message = jnp.stack([jnp.concatenate([part, shared], 1) for part in queries])
        message = jnp.roll(message, b, axis=0)
        arrived = lax.all_to_all(message, "zb", 0, 0, tiled=True)
        total = jnp.sum(arrived.astype(F32), axis=0)
        inverse = lax.rsqrt(jnp.sum(total[:, 4 * HD :], axis=1, keepdims=True) / D + 1e-05)
        total = total[:, : 4 * HD] * inverse
        key_rows = rotate(total[:, 2 * HD : 3 * HD], cosine, sine).astype(BF16)
        value_rows = total[:, 3 * HD :].astype(BF16)
        heads = []
        for head in range(2):
            query_rows = rotate(total[:, head * HD : (head + 1) * HD], cosine, sine).astype(BF16)
            scores = jnp.dot(query_rows, key_rows.T, preferred_element_type=F32) * scale
            scores = jnp.where(allowed[lap_step], scores, -jnp.inf)
            weights = jnp.exp(scores - jnp.max(scores, axis=-1, keepdims=True))
            probs = (weights / jnp.sum(weights, axis=-1, keepdims=True)).astype(BF16)
            heads.append(jnp.dot(probs, value_rows, preferred_element_type=F32).astype(BF16))
        attended = in_order(heads[0], heads[1], y, 1)
        if lap_step in (1, 2):
            attended = lax.all_to_all(to_all(attended, GROUP * GROUP), ("za", "zb"), 0, 0, tiled=True)
            attended = attended.transpose(1, 0, 2).reshape(MB_ROWS, GROUP * GROUP * 2 * HD)
        else:
            attended = lax.all_gather(attended, ("za", "zb"), axis=1, tiled=True)
        projected = jnp.dot(attended, w_o_pair, preferred_element_type=F32)
        state_wide = state.astype(F32)
        if lap_step < STEPS - 1:
            update = in_order(projected[:, :COLS], projected[:, COLS:], y, 1)
            state = shift((state_wide + update).astype(BF16), "section", 1)
    low, high = state_wide[:, :COLS], state_wide[:, COLS:]
    own = (jnp.where(y == 0, low, high) + projected[:, :COLS]).astype(BF16)
    other = (jnp.where(y == 0, high, low) + projected[:, COLS:]).astype(BF16)
    crossing = [(2 * i + j, 2 * ((i + 1) % stops) + 1 - j) for i in range(stops) for j in range(2)]
    own = shift(own, "section", 1)
    other = lax.ppermute(other, ("section", "y"), crossing)
    return in_order(own, other, y, 0)


def solution(mesh):
    sections = mesh.shape["section"]
    parts = mesh.shape["tensor"]
    names = ("section", "za", "zb", "y")
    fine = Mesh(mesh.devices.reshape(sections, parts // (2 * GROUP), GROUP, 2), names)
    tensor = names[1:]
    in_specs = (
        P("section", tensor),
        P("section", tensor),
        P(),
        P(),
        P("section", tensor),
        P("section", None, tensor),
        P("section", tensor, None),
        P("section", None, tensor),
    )
    return jax.shard_map(local, mesh=fine, in_specs=in_specs, out_specs=P("section", tensor), check_vma=False)
```

```python
import math

import jax
import jax.numpy as jnp
from jax import lax
from jax.sharding import Mesh
from jax.sharding import PartitionSpec as P

D = 8192
HD = 128
KVH = 4
MB_DEV = 2
AUD_MB = 32
TXT_MB = 32
AUD_DEV = 32
STEPS = 4
MB_ROWS = 64
CAP = 4
COLS = 256
GROUP = 4
F32 = jnp.float32
BF16 = jnp.bfloat16


def shift(block, axis, distance):
    count = lax.axis_size(axis)
    return lax.ppermute(block, axis, [(i, (i + distance) % count) for i in range(count)])


def rotate(values, cosine, sine):
    half = values.shape[-1] // 2
    first = values[..., :half]
    second = values[..., half:]
    return jnp.concatenate([first * cosine - second * sine, second * cosine + first * sine], -1)


def rope_tables(rows, width):
    position = jnp.arange(rows, dtype=F32)
    freq = 500000.0 ** (-(2.0 * jnp.arange(width // 2, dtype=F32)) / width)
    angle = position[:, None] * freq[None, :]
    return (jnp.cos(angle), jnp.sin(angle))


def pick(stack, index, axis):
    return lax.dynamic_index_in_dim(stack, index, axis, keepdims=False)


def to_all(block, count):
    return jnp.broadcast_to(block[None], (count,) + block.shape)


def split_float(values):
    coarse = values.astype(BF16)
    rest = values - coarse.astype(F32)
    middle = rest.astype(BF16)
    lane = jnp.arange(HD, dtype=jnp.int32)[None, :]
    fine = (rest - middle.astype(F32)).astype(BF16)
    zero = jnp.zeros((), BF16)
    return jnp.where(lane == 0, coarse, jnp.where(lane == 1, middle, jnp.where(lane == 2, fine, zero)))


def in_order(own, other, y, axis):
    first = jnp.where(y == 0, own, other)
    second = jnp.where(y == 0, other, own)
    return jnp.concatenate([first, second], axis)


def local(hidden, audio, audio_dest, segment, norm_gain, w_query, w_keyval, w_out):
    stops = lax.axis_size("section")
    s = lax.axis_index("section")
    a = lax.axis_index("za")
    b = lax.axis_index("zb")
    y = lax.axis_index("y")

    features = GROUP * 2 * COLS
    w_q = w_query[0].reshape(GROUP, GROUP, 2 * COLS, HD)
    parts = [pick(w_q, (b - j) % GROUP, 1).reshape(features, HD) for j in range(GROUP)]
    group_own = [shift(part, "zb", -j) if j else part for j, part in enumerate(parts)]

    text = hidden.reshape(MB_DEV, TXT_MB, COLS)
    gain_rows = jnp.broadcast_to(norm_gain, (16, COLS))

    def batch(index):
        return jnp.concatenate([pick(text, index, 0), gain_rows], 0)

    written = in_order(batch(y), shift(batch(1 - y), "y", 1), y, 1)
    targets = audio_dest[:, 0].reshape(stops, AUD_DEV)
    half_stops = stops // MB_DEV

    order = jnp.arange(AUD_DEV, dtype=jnp.int32)
    own_targets = pick(targets, s, 0)
    rank = jnp.sum(
        ((own_targets[:, None] == own_targets[None, :]) & (order[None, :] < order[:, None])).astype(jnp.int32),
        axis=1,
    )
    holder = 2 * own_targets + s // half_stops
    seats = jnp.arange(stops * MB_DEV * CAP, dtype=jnp.int32)
    chosen = seats[:, None] == (holder * CAP + rank)[None, :]
    outgoing = jnp.dot(chosen.astype(BF16), audio, preferred_element_type=F32).astype(BF16)
    slots = lax.all_to_all(outgoing.reshape(stops * MB_DEV, CAP, COLS), ("section", "y"), 0, 0, tiled=True)
    slots = pick(slots.reshape(MB_DEV, half_stops, 2, CAP, COLS), y, 0)
    slots = slots.transpose(0, 2, 1, 3).reshape(AUD_MB, 2 * COLS)

    both = jnp.concatenate([slots, written], 0)
    first_other = shift(parts[0], "y", 1)
    both, group_own, first_other, w_kv = lax.optimization_barrier((both, group_own, first_other, w_keyval[0]))
    state = both[:MB_ROWS]
    group_other = shift(jnp.stack(group_own[1:3]), "y", 1)
    w_kv = w_kv.reshape(COLS, GROUP, 2 * HD).transpose(1, 0, 2)
    kv_own = lax.all_to_all(w_kv, "za", 0, 0, tiled=True)
    both, kv_own = lax.optimization_barrier((both, kv_own))
    kv_flat = kv_own.reshape(GROUP * COLS, 2 * HD)
    kv_flat = jnp.concatenate([kv_flat[:, :HD], kv_flat[:, HD:]], 0)
    last = shift(jnp.stack([group_own[3], kv_flat]), "y", 1)
    kv_other = jnp.concatenate([last[1, : GROUP * COLS], last[1, GROUP * COLS :]], 1).reshape(kv_own.shape)
    w_kv_rows = in_order(kv_own, kv_other, y, 1).reshape(features, 2 * HD)
    group_other = [first_other, group_other[0], group_other[1], last[0]]
    w_group = [jnp.concatenate([mine, others], 1) for mine, others in zip(group_own, group_other)]
    w_group = lax.optimization_barrier(w_group)

    seat_ids = jnp.arange(AUD_MB, dtype=jnp.int32)
    owner = y * (AUD_MB // CAP) + seat_ids // CAP
    row_ids = jnp.arange(MB_ROWS, dtype=jnp.int32)
    causal = row_ids[None, :] <= row_ids[:, None]
    diagonal = row_ids[None, :] == row_ids[:, None]
    allowed = []
    for lap_step in range(STEPS):
        root = (s - lap_step) % stops
        clip = pick(segment, root * MB_DEV + y, 0)
        counts = jnp.sum((targets == root).astype(jnp.int32), axis=1)
        held = jnp.sum(
            jnp.where(owner[:, None] == jnp.arange(stops, dtype=jnp.int32)[None, :], counts[None, :], 0), axis=1
        )
        live = jnp.concatenate([seat_ids % CAP < held, jnp.ones((TXT_MB,), jnp.bool_)], 0)
        allowed.append(causal & (clip[:, None] == clip[None, :]) & (live[None, :] | diagonal))
    cosine, sine = rope_tables(MB_ROWS, HD)
    scale = 1.0 / math.sqrt(HD)

    for lap_step in range(STEPS):
        if lap_step == 0:
            wide = lax.all_gather(both, "za", axis=1, tiled=True)
            wide, w_o = lax.optimization_barrier((wide, w_out[0]))
            middle = w_o.shape[0] // 2
            w_o_upper = shift(w_o[:middle], "y", 1)
            gain_wide = wide[MB_ROWS : MB_ROWS + 1].astype(F32)
            wide = wide[:MB_ROWS].astype(F32)
        else:
            wide = lax.all_gather(state, "za", axis=1, tiled=True).astype(F32)
        scaled = (wide * gain_wide).astype(BF16)
        squares = jnp.sum(wide * wide, axis=1, keepdims=True)
        queries = [jnp.dot(scaled, part, preferred_element_type=F32).astype(BF16) for part in w_group]
        key_values = jnp.dot(scaled, w_kv_rows, preferred_element_type=F32).astype(BF16)
        shared = jnp.concatenate([key_values, split_float(squares)], 1)
        message = jnp.stack([jnp.concatenate([part, shared], 1) for part in queries])
        message = jnp.roll(message, b, axis=0)
        arrived = lax.all_to_all(message, "zb", 0, 0, tiled=True)
        if lap_step == 0:
            arrived, w_o_upper = lax.optimization_barrier((arrived, w_o_upper))
            w_o_other = jnp.concatenate([w_o_upper, shift(w_o[middle:], "y", 1)], 0)
            w_o_pair = lax.optimization_barrier(jnp.concatenate([w_out[0], w_o_other], 1))
        total = jnp.sum(arrived.astype(F32), axis=0)
        inverse = lax.rsqrt(jnp.sum(total[:, 4 * HD :], axis=1, keepdims=True) / D + 1e-05)
        total = total[:, : 4 * HD] * inverse
        key_rows = rotate(total[:, 2 * HD : 3 * HD], cosine, sine).astype(BF16)
        value_rows = total[:, 3 * HD :].astype(BF16)
        heads = []
        for head in range(2):
            query_rows = rotate(total[:, head * HD : (head + 1) * HD], cosine, sine).astype(BF16)
            scores = jnp.dot(query_rows, key_rows.T, preferred_element_type=F32) * scale
            scores = jnp.where(allowed[lap_step], scores, -jnp.inf)
            weights = jnp.exp(scores - jnp.max(scores, axis=-1, keepdims=True))
            probs = (weights / jnp.sum(weights, axis=-1, keepdims=True)).astype(BF16)
            heads.append(jnp.dot(probs, value_rows, preferred_element_type=F32).astype(BF16))
        attended = in_order(heads[0], heads[1], y, 1)
        if lap_step in (1, 2):
            attended = lax.all_to_all(to_all(attended, GROUP * GROUP), ("za", "zb"), 0, 0, tiled=True)
            attended = attended.transpose(1, 0, 2).reshape(MB_ROWS, GROUP * GROUP * 2 * HD)
        else:
            attended = lax.all_gather(attended, ("za", "zb"), axis=1, tiled=True)
        projected = jnp.dot(attended, w_o_pair, preferred_element_type=F32)
        state_wide = state.astype(F32)
        if lap_step < STEPS - 1:
            update = in_order(projected[:, :COLS], projected[:, COLS:], y, 1)
            state = shift((state_wide + update).astype(BF16), "section", 1)
    low, high = state_wide[:, :COLS], state_wide[:, COLS:]
    own = (jnp.where(y == 0, low, high) + projected[:, :COLS]).astype(BF16)
    other = (jnp.where(y == 0, high, low) + projected[:, COLS:]).astype(BF16)
    crossing = [(2 * i + j, 2 * ((i + 1) % stops) + 1 - j) for i in range(stops) for j in range(2)]
    own = shift(own, "section", 1)
    other = lax.ppermute(other, ("section", "y"), crossing)
    return in_order(own, other, y, 0)


def solution(mesh):
    sections = mesh.shape["section"]
    parts = mesh.shape["tensor"]
    names = ("section", "za", "zb", "y")
    fine = Mesh(mesh.devices.reshape(sections, parts // (2 * GROUP), GROUP, 2), names)
    tensor = names[1:]
    in_specs = (
        P("section", tensor),
        P("section", tensor),
        P(),
        P(),
        P("section", tensor),
        P("section", None, tensor),
        P("section", tensor, None),
        P("section", None, tensor),
    )
    return jax.shard_map(local, mesh=fine, in_specs=in_specs, out_specs=P("section", tensor), check_vma=False)
```
